128 devices in a mesh: row: 16 (over x, z), col: 8 (over y, core).
Axes of the slice: x: 4, y: 4, z: 4, core: 2. Of those that a mesh axis runs over, the one named last changes fastest.
Arguments:
- tokens: bfloat16 [1024, 6144], P('col', 'row'), may hold values from -6 to 6
- in_codes: bfloat16 [6144, 24576], P('row', 'col'), may hold values from -6 to 6
- in_scales: float32 [48, 192], P('row', 'col'), may hold values from 0.0038273276 to 0.03827328
- out_codes: bfloat16 [24576, 6144], P('col', 'row'), may hold values from -6 to 6
- out_scales: float32 [192, 48], P('col', 'row'), may hold values from 0.0019136638 to 0.01913664
- out_grad: bfloat16 [1024, 6144], P('col', 'row'), may hold values from -6 to 6
Outputs:
- block_out: bfloat16 [1024, 6144], P('col', 'row')
- tokens_grad: bfloat16 [1024, 6144], P('col', 'row')
- in_grad: float32 [6144, 24576], P('row', 'col')
- out_grad_weight: float32 [24576, 6144], P('col', 'row')
The draws below stay inside these ranges and needn't reach their ends.
All inputs are finite; a program needn't handle non-finite values.
Results may differ from the reference program's by a relative error of at most 0.0071.
Values may be sent and summed in bfloat16 or wider, within the bound.
No kernel may reach another device: no remote copies, remote signals or barrier semaphores. Data moves between devices by JAX's collectives and lax.ppermute only.
A program may use at most 192 MiB of HBM per device.

```python
import math
import jax
import jax.numpy as jnp

D = 6144
FF = 24576
BLK = 128
TOKENS = 1024


def shard_levels(own_key, shape, split, smallest, largest):
    level, own = 1.0, jax.random.fold_in(own_key, 6)
    for position, shards_of in split:
        heights = jnp.exp(jax.random.uniform(jax.random.fold_in(own, position), (shards_of,), jnp.float32, smallest / len(split), largest / len(split)))
        level = level * jnp.repeat(heights, shape[position] // shards_of).reshape([-1 if axis == position else 1 for axis in range(len(shape))])
    return level


def gaussian(rng, dims, width, bound, split=(), kind=jnp.bfloat16):
    factor_of = shard_levels(rng, dims, split, -0.22, 0.18) if split else 1.0
    drawn = jax.random.normal(rng, dims, jnp.float32) * width * factor_of
    return jnp.minimum(jnp.maximum(drawn, -bound), bound).astype(kind)


def setup_inputs(seed: int = 0) -> dict:
    streams_of = jax.random.split(jax.random.key(seed), 7)
    return {
        "tokens": gaussian(streams_of[0], (TOKENS, D), 1.0, 6.0, ((0, 8), (1, 16))),
        "in_codes": gaussian(streams_of[1], (D, FF), 1.0, 6.0, ((0, 16), (1, 8))),
        "in_scales": jnp.clip(jnp.exp(math.log(0.03827328) - 2.3025852 * jax.random.uniform(streams_of[2], (D // BLK, FF // BLK), jnp.float32) ** shard_levels(streams_of[2], (D // BLK, FF // BLK), ((0, 16), (1, 8)), -0.2, 0.2)), 0.0038273276, 0.03827328),
        "out_codes": gaussian(streams_of[3], (FF, D), 1.0, 6.0, ((0, 8), (1, 16))),
        "out_scales": jnp.clip(jnp.exp(math.log(0.01913664) - 2.3025852 * jax.random.uniform(streams_of[4], (FF // BLK, D // BLK), jnp.float32) ** shard_levels(streams_of[4], (FF // BLK, D // BLK), ((0, 8), (1, 16)), -0.2, 0.2)), 0.0019136638, 0.01913664),
        "out_grad": gaussian(streams_of[5], (TOKENS, D), 1.0, 6.0, ((0, 8), (1, 16))),
    }


def dequant(codes, scales):
    rows, cols = codes.shape
    wide = codes.astype(jnp.float32).reshape(rows // BLK, BLK, cols // BLK, BLK) * scales[:, None, :, None]
    return wide.reshape(rows, cols).astype(jnp.bfloat16)


def gelu_value(value):
    return 0.5 * value * (1.0 + jax.scipy.special.erf(value * 0.7071067811865476))


def gelu_slope(value):
    cumul = 0.5 * (1.0 + jax.scipy.special.erf(value * 0.7071067811865476))
    return cumul + value * jnp.exp(-0.5 * value * value) * 0.3989422804014327


def reference(tokens, in_codes, in_scales, out_codes, out_scales, out_grad):
    w_in = dequant(in_codes, in_scales)
    w_out = dequant(out_codes, out_scales)
    pre = jnp.dot(tokens, w_in, preferred_element_type=jnp.float32)
    act = gelu_value(pre).astype(jnp.bfloat16)
    block_out = jnp.dot(act, w_out, preferred_element_type=jnp.float32).astype(jnp.bfloat16)
    act_grad = jnp.dot(out_grad, w_out.T, preferred_element_type=jnp.float32)
    pre_grad = (act_grad * gelu_slope(pre)).astype(jnp.bfloat16)
    tokens_grad = jnp.dot(pre_grad, w_in.T, preferred_element_type=jnp.float32).astype(jnp.bfloat16)
    in_grad = jnp.dot(tokens.T, pre_grad, preferred_element_type=jnp.float32)
    out_grad_weight = jnp.dot(act.T, out_grad, preferred_element_type=jnp.float32)
    return block_out, tokens_grad, in_grad, out_grad_weight
```

```python
import functools

import jax
import jax.numpy as jnp
from jax import lax
from jax.experimental import pallas as pl
from jax.experimental.pallas import tpu as pltpu
from jax.sharding import Mesh, PartitionSpec as P

BLK = 128
RING = 4
BF16, F32 = jnp.bfloat16, jnp.float32
VMEM_LIMIT = 56 * 1024 * 1024


def gelu_value(value):
    return 0.5 * value * (1.0 + lax.erf(value * 0.7071067811865476))


def gelu_slope(value):
    cumul = 0.5 * (1.0 + lax.erf(value * 0.7071067811865476))
    return cumul + value * jnp.exp(-0.5 * value * value) * 0.3989422804014327


def shift(value, axis, step):
    size = 2 if axis == "c" else RING
    return lax.ppermute(value, axis, [(i, (i + step) % size) for i in range(size)])


def dot(left, right, dims=((1,), (0,))):
    return lax.dot_general(left, right, (dims, ((), ())), preferred_element_type=F32)


def whole(shape):
    return pl.BlockSpec(shape, lambda i, ids: (0,) * len(shape))


def call(body, ids, args, in_specs, out_shape, out_specs, flops, moved):
    return pl.pallas_call(
        body,
        grid_spec=pltpu.PrefetchScalarGridSpec(
            num_scalar_prefetch=1, grid=(RING,), in_specs=in_specs, out_specs=out_specs
        ),
        out_shape=out_shape,
        compiler_params=pltpu.CompilerParams(
            dimension_semantics=("arbitrary",), vmem_limit_bytes=VMEM_LIMIT
        ),
        cost_estimate=pl.CostEstimate(flops=flops, bytes_accessed=moved, transcendentals=0),
    )(ids, *args)


def at_step(step, refs, write):
    for index, ref in enumerate(refs):
        pl.when(step == index)(functools.partial(write, ref))


def dequant(ids, codes, scales, by_columns):
    rows, cols = codes.shape
    block = (rows, cols // RING) if by_columns else (rows // RING, cols)
    high, wide = block[0] // BLK, block[1] // BLK

    def body(ids_ref, scale_ref, code_ref, *outs):
        step = pl.program_id(0)
        quarter = lax.rem(ids_ref[1] + step, RING)

        def write(out):
            for a in range(high):
                for b in range(wide):
                    place = (slice(a * BLK, (a + 1) * BLK), slice(b * BLK, (b + 1) * BLK))
                    if by_columns:
                        scale = scale_ref[a, quarter * wide + b]
                    else:
                        scale = scale_ref[quarter * high + a, b]
                    out[place] = (code_ref[place].astype(F32) * scale).astype(BF16)

        at_step(step, outs, write)

    if by_columns:
        where = lambda i, ids: (0, lax.rem(ids[1] + i, RING))
    else:
        where = lambda i, ids: (lax.rem(ids[1] + i, RING), 0)
    return call(
        body, ids, (scales, codes),
        [pl.BlockSpec(memory_space=pltpu.SMEM), pl.BlockSpec(block, where)],
        [jax.ShapeDtypeStruct(block, BF16)] * RING, [whole(block)] * RING,
        rows * cols, 4 * rows * cols,
    )


def hidden(ids, own, other, tiles, transposed):
    _, _, rows, depth = own.shape
    width = tiles[0].shape[0 if transposed else 1]
    dims = ((1,), (1,)) if transposed else ((1,), (0,))

    def body(ids_ref, own_ref, other_ref, *refs):
        weights, outs = refs[:RING], refs[RING:]
        total = None
        for k in range(RING):
            left = jnp.concatenate([own_ref[0, k], other_ref[0, k]], axis=0)
            part = dot(left, weights[k][...], dims)
            total = part if total is None else total + part

        def write(out):
            out[...] = total.astype(out.dtype)

        at_step(pl.program_id(0), outs, write)

    block = (1, RING, rows, depth)
    where = lambda i, ids: (lax.rem(ids[0] + i, RING), 0, 0, 0)
    shape = (2 * rows, width)
    return call(
        body, ids, (own, other, *tiles),
        [pl.BlockSpec(block, where)] * 2 + [whole(t.shape) for t in tiles],
        [jax.ShapeDtypeStruct(shape, F32)] + [jax.ShapeDtypeStruct(shape, BF16)] * 3,
        [whole(shape)] * RING,
        2 * RING * RING * shape[0] * depth * width, 4 * own.size + 8 * tiles[0].size + 8 * shape[0] * width,
    )


def model(ids, parts, tiles, transposed):
    rows = parts[0].shape[0] // 2
    depth = tiles[0].shape[0 if transposed else 1]
    dims = ((1,), (1,)) if transposed else ((1,), (0,))

    def body(ids_ref, *refs):
        lefts, weights, (keep, send) = refs[:RING], refs[RING:2 * RING], refs[2 * RING:]

        def write(left):
            for k in range(RING):
                total = dot(left[...], weights[k][...], dims)
                keep[0, k] = total[:rows].astype(keep.dtype)
                send[0, k] = total[rows:].astype(send.dtype)

        at_step(pl.program_id(0), lefts, write)

    block = (1, RING, rows, depth)
    where = lambda i, ids: (lax.rem(ids[0] + RING - i, RING), 0, 0, 0)
    shape = (RING, RING, rows, depth)
    return call(
        body, ids, (*parts, *tiles),
        [whole(p.shape) for p in parts] + [whole(t.shape) for t in tiles],
        [jax.ShapeDtypeStruct(shape, F32), jax.ShapeDtypeStruct(shape, BF16)],
        [pl.BlockSpec(block, where)] * 2,
        2 * RING * RING * parts[0].size * depth, 8 * parts[0].size + 8 * tiles[0].size + 96 * rows * depth,
    )


def weight_grad(ids, own, other, parts, model_first):
    _, _, rows, depth = own.shape
    width = parts[0].shape[1]
    shape = (depth, width) if model_first else (width, depth)

    def body(ids_ref, own_ref, other_ref, *refs):
        hid, outs = refs[:RING], refs[RING:]
        step = pl.program_id(0)
        total = None
        for k in range(RING):
            quarter = lax.rem(ids_ref[0] + RING - k, RING)
            wide = jnp.concatenate([own_ref[quarter, step], other_ref[quarter, step]], axis=0)
            pair = (wide, hid[k][...]) if model_first else (hid[k][...], wide)
            part = dot(*pair, ((0,), (0,)))
            total = part if total is None else total + part

        def write(out):
            out[...] = total.astype(out.dtype)

        at_step(step, outs, write)

    return call(
        body, ids, (own, other, *parts),
        [whole(own.shape)] * 2 + [whole(p.shape) for p in parts],
        [jax.ShapeDtypeStruct(shape, F32)] + [jax.ShapeDtypeStruct(shape, BF16)] * 3,
        [whole(shape)] * RING,
        2 * RING * RING * parts[0].size * depth, 4 * own.size + 8 * parts[0].size + 10 * depth * width,
    )


def assemble(ids, parts, by_columns):
    rows, cols = parts[0].shape

    def body(ids_ref, *refs):
        out = refs[RING]

        def write(part):
            out[...] = part[...].astype(F32)

        at_step(pl.program_id(0), refs[:RING], write)

    if by_columns:
        shape, where = (rows, RING * cols), lambda i, ids: (0, lax.rem(ids[1] + i, RING))
    else:
        shape, where = (RING * rows, cols), lambda i, ids: (lax.rem(ids[1] + i, RING), 0)
    return call(
        body, ids, parts, [whole(p.shape) for p in parts],
        jax.ShapeDtypeStruct(shape, F32), pl.BlockSpec((rows, cols), where),
        rows * cols * RING, 26 * rows * cols,
    )


def gather(value):
    along_z = jnp.stack([value] + [shift(value, "z", k) for k in range(1, RING)])
    own = jnp.stack([along_z] + [shift(along_z, "y", k) for k in range(1, RING)])
    return own, shift(own, "c", 1)


def reduce_hidden(parts):
    total = parts[0]
    for k in range(1, RING):
        total = total + shift(parts[k], "x", k).astype(F32)
    return total


def gather_hidden(value):
    return [value] + [shift(value, "x", k) for k in range(1, RING)]


def reduce_model(keep, send):
    got = shift(send, "c", 1)
    along_y = keep[0] + got[0].astype(F32)
    for k in range(1, RING):
        along_y = along_y + shift((keep[k] + got[k].astype(F32)).astype(BF16), "y", RING - k).astype(F32)
    total = along_y[0]
    for k in range(1, RING):
        total = total + shift(along_y[k].astype(BF16), "z", RING - k).astype(F32)
    return total.astype(BF16)


def scatter_weight(ids, parts, by_columns):
    moved = [parts[0]] + [shift(parts[k], "z", RING - k) for k in range(1, RING)]
    return assemble(ids, moved, by_columns)


def spread_tiles(tiles):
    return [tiles[0]] + [shift(tiles[k], "z", k) for k in range(1, RING)]


def local(tokens, in_codes, in_scales, out_codes, out_scales, out_grad):
    ids = jnp.stack([lax.axis_index(name).astype(jnp.int32) for name in ("x", "z")])
    w_in = spread_tiles(dequant(ids, in_codes, in_scales, True))
    tok = gather(tokens)
    w_out = spread_tiles(dequant(ids, out_codes, out_scales, False))
    grad = gather(out_grad)
    pre = reduce_hidden(hidden(ids, *tok, w_in, False))
    act = gather_hidden(gelu_value(pre).astype(BF16))
    act_grad = reduce_hidden(hidden(ids, *grad, w_out, True))
    pre_grad = gather_hidden((act_grad * gelu_slope(pre)).astype(BF16))
    out_grad_weight = scatter_weight(ids, weight_grad(ids, *grad, act, False), False)
    block_out = reduce_model(*model(ids, act, w_out, False))
    tokens_grad = reduce_model(*model(ids, pre_grad, w_in, True))
    in_grad = scatter_weight(ids, weight_grad(ids, *tok, pre_grad, True), True)
    return block_out, tokens_grad, in_grad, out_grad_weight


def solution(mesh):
    grid = Mesh(mesh.devices.reshape(RING, RING, RING, 2), ("x", "z", "y", "c"))
    row, col = ("x", "z"), ("y", "c")
    in_specs = (P(col, row), P(row, col), P(row, col), P(col, row), P(col, row), P(col, row))
    out_specs = (P(col, row), P(col, row), P(row, col), P(col, row))
    return jax.shard_map(local, mesh=grid, in_specs=in_specs, out_specs=out_specs, check_vma=False)
```

```python
import functools

import jax
import jax.numpy as jnp
from jax import lax
from jax.experimental import pallas as pl
from jax.experimental.pallas import tpu as pltpu
from jax.sharding import Mesh, PartitionSpec as P

BLK = 128
RING = 4
BF16, F32 = jnp.bfloat16, jnp.float32
VMEM_LIMIT = 56 * 1024 * 1024


def gelu_value(value):
    return 0.5 * value * (1.0 + lax.erf(value * 0.7071067811865476))


def gelu_slope(value):
    cumul = 0.5 * (1.0 + lax.erf(value * 0.7071067811865476))
    return cumul + value * jnp.exp(-0.5 * value * value) * 0.3989422804014327


def shift(value, axis, step):
    size = 2 if axis == "c" else RING
    return lax.ppermute(value, axis, [(i, (i + step) % size) for i in range(size)])


def dot(left, right, dims=((1,), (0,))):
    return lax.dot_general(left, right, (dims, ((), ())), preferred_element_type=F32)


def whole(shape):
    return pl.BlockSpec(shape, lambda i, ids: (0,) * len(shape))


def call(body, ids, grid, args, in_specs, out_shape, out_specs, scratch, flops, moved):
    return pl.pallas_call(
        body,
        grid_spec=pltpu.PrefetchScalarGridSpec(
            num_scalar_prefetch=1, grid=grid, in_specs=in_specs, out_specs=out_specs, scratch_shapes=scratch
        ),
        out_shape=out_shape,
        compiler_params=pltpu.CompilerParams(
            dimension_semantics=("arbitrary",), vmem_limit_bytes=VMEM_LIMIT
        ),
        cost_estimate=pl.CostEstimate(flops=0, bytes_accessed=0, transcendentals=0),
    )(ids, *args)


def at_step(step, refs, write):
    for index, ref in enumerate(refs):
        pl.when(step == index)(functools.partial(write, ref))


def after(value, *others):
    return lax.optimization_barrier((value, *others))[0]


def dequant(ids, codes, scales, by_columns):
    rows, cols = codes.shape
    block = (rows, cols // RING) if by_columns else (rows // RING, cols)
    high, wide = block[0] // BLK, block[1] // BLK

    def body(ids_ref, scale_ref, code_ref, out):
        quarter = pl.program_id(0)
        for a in range(high):
            for b in range(wide):
                place = (slice(a * BLK, (a + 1) * BLK), slice(b * BLK, (b + 1) * BLK))
                scale = scale_ref[a, quarter * wide + b] if by_columns else scale_ref[quarter * high + a, b]
                out[(0, *place)] = (code_ref[place].astype(F32) * scale).astype(BF16)

    return call(
        body, ids, (RING,), (scales, codes),
        [pl.BlockSpec(memory_space=pltpu.SMEM),
         pl.BlockSpec(block, lambda i, ids: (0, i) if by_columns else (i, 0))],
        jax.ShapeDtypeStruct((RING, *block), BF16), pl.BlockSpec((1, *block), lambda i, ids: (i, 0, 0)), [],
        rows * cols, 4 * rows * cols,
    )


def hidden(ids, own, other, tiles, transposed):
    _, _, rows, depth = own.shape
    width = tiles.shape[1 if transposed else 2]
    step = 2 * BLK
    dims = ((1,), (1,)) if transposed else ((1,), (0,))

    def fill(ids_ref, own_ref, other_ref, left_ref):
        for k in range(RING):
            start = pl.multiple_of(lax.rem(ids_ref[1] + RING - k, RING) * depth, depth)
            for s, half in enumerate((own_ref, other_ref)):
                left_ref[pl.ds(s * RING * rows, RING * rows), pl.ds(start, depth)] = half[:, k].reshape(RING * rows, depth)

    def body(ids_ref, own_ref, other_ref, tile_ref, *refs):
        outs, left_ref, total_ref = refs[:RING], refs[RING], refs[RING + 1]
        pl.when(pl.program_id(0) == 0)(lambda: fill(ids_ref, own_ref, other_ref, left_ref))
        if transposed:
            right = jnp.concatenate([tile_ref[z] for z in range(RING)], axis=1)
        else:
            right = tile_ref[...].reshape(RING * depth, step)
        total_ref[...] = dot(left_ref[...], right, dims).reshape(2, RING, rows, step)
        for k in range(RING):
            quarter = lax.rem(ids_ref[0] + k, RING)
            for s in range(2):
                outs[k][s] = total_ref[s, quarter].astype(outs[k].dtype)

    tile_spec = (
        pl.BlockSpec((RING, step, depth), lambda i, ids: (0, i, 0)) if transposed
        else pl.BlockSpec((RING, depth, step), lambda i, ids: (0, 0, i))
    )
    shape = (2, rows, width)
    return call(
        body, ids, (width // step,), (own, other, tiles),
        [whole(own.shape)] * 2 + [tile_spec],
        [jax.ShapeDtypeStruct(shape, F32)] + [jax.ShapeDtypeStruct(shape, BF16)] * 3,
        [pl.BlockSpec((2, rows, step), lambda i, ids: (0, 0, i))] * RING,
        [pltpu.VMEM((2 * RING * rows, RING * depth), BF16), pltpu.VMEM((2, RING, rows, step), F32)],
        4 * own.size * width, 4 * own.size + 2 * tiles.size + 20 * rows * width,
    )


def place_parts(ids_ref, parts, whole_ref):
    rows = parts[0].shape[1]
    for k, part in enumerate(parts):
        quarter = lax.rem(ids_ref[0] + RING - k, RING)
        for s in range(2):
            whole_ref[pl.ds(pl.multiple_of((s * RING + quarter) * rows, rows), rows), :] = part[s]


def model(ids, parts, tiles, transposed):
    _, rows, width = parts[0].shape
    tokens = 2 * RING * rows
    depth = tiles.shape[1 if transposed else 2]
    dims = ((1,), (1,)) if transposed else ((1,), (0,))

    def body(ids_ref, *refs):
        hid, (tile_ref, keep, send, hid_ref) = refs[:RING], refs[RING:]
        pl.when(pl.program_id(0) == 0)(lambda: place_parts(ids_ref, hid, hid_ref))
        total = dot(hid_ref[...], tile_ref[0], dims).reshape(2, RING, rows, depth)
        keep[0] = total[0]
        send[0] = total[1].astype(send.dtype)

    shape = (RING, RING, rows, depth)
    out_spec = pl.BlockSpec((1, RING, rows, depth), lambda i, ids: (i, 0, 0, 0))
    return call(
        body, ids, (RING,), (*parts, tiles),
        [whole(p.shape) for p in parts]
        + [pl.BlockSpec((1, *tiles.shape[1:]), lambda i, ids: (lax.rem(ids[1] + RING - i, RING), 0, 0))],
        [jax.ShapeDtypeStruct(shape, F32), jax.ShapeDtypeStruct(shape, BF16)],
        [out_spec] * 2,
        [pltpu.VMEM((tokens, width), BF16)],
        2 * RING * tokens * width * depth, 2 * tokens * width + 2 * tiles.size + 12 * tokens * depth,
    )


def weight_grad(ids, own, other, parts, model_first):
    _, _, rows, depth = own.shape
    width = parts[0].shape[2]
    tokens = 2 * RING * rows
    shape = (depth, width) if model_first else (width, depth)

    def body(ids_ref, own_ref, other_ref, *refs):
        hid, (out, hid_ref) = refs[:RING], refs[RING:]
        pl.when(pl.program_id(0) == 0)(lambda: place_parts(ids_ref, hid, hid_ref))
        wide = jnp.concatenate([half[:, 0].reshape(RING * rows, depth) for half in (own_ref, other_ref)], axis=0)
        pair = (wide, hid_ref[...]) if model_first else (hid_ref[...], wide)
        out[0] = dot(*pair, ((0,), (0,))).astype(out.dtype)

    return call(
        body, ids, (RING,), (own, other, *parts),
        [pl.BlockSpec((RING, 1, rows, depth), lambda i, ids: (0, lax.rem(ids[1] + RING - i, RING), 0, 0))] * 2
        + [whole(p.shape) for p in parts],
        jax.ShapeDtypeStruct((RING, *shape), BF16), pl.BlockSpec((1, *shape), lambda i, ids: (i, 0, 0)),
        [pltpu.VMEM((tokens, width), BF16)],
        2 * RING * tokens * width * depth, 4 * own.size + 2 * tokens * width + 8 * depth * width,
    )


def assemble(ids, blocks, by_columns):
    _, rows, cols = blocks.shape

    def body(ids_ref, block_ref, out):
        out[...] = block_ref[0].astype(F32)

    shape = (rows, RING * cols) if by_columns else (RING * rows, cols)
    return call(
        body, ids, (RING,), (blocks,),
        [pl.BlockSpec((1, rows, cols), lambda i, ids: (i, 0, 0))],
        jax.ShapeDtypeStruct(shape, F32),
        pl.BlockSpec((rows, cols), lambda i, ids: (0, i) if by_columns else (i, 0)), [],
        blocks.size, 6 * blocks.size,
    )


def along_z(value):
    return jnp.stack([value] + [shift(value, "z", k) for k in range(1, RING)], axis=1)


def along_y(value):
    moved = [shift(value, "y", k) for k in range(1, RING)]
    own = jnp.stack([value] + moved)
    return own, shift(own, "c", 1), moved[0]


def swap_hidden(parts):
    return [parts[0]] + [shift(parts[k], "x", k) for k in range(1, RING)]


def gather_hidden(value):
    return [value] + [shift(value, "x", k) for k in range(1, RING)]


def add(parts):
    total = parts[0].astype(F32)
    for part in parts[1:]:
        total = total + part.astype(F32)
    return total


def reduce_model(keep, send):
    got = shift(send, "c", 1)
    along_y = keep[:, 0] + got[:, 0].astype(F32)
    for j in range(1, RING):
        along_y = along_y + shift((keep[:, j] + got[:, j].astype(F32)).astype(BF16), "y", RING - j).astype(F32)
    total = along_y[0]
    for k in range(1, RING):
        total = total + shift(along_y[k].astype(BF16), "z", RING - k).astype(F32)
    return total.astype(BF16)


def swap_z(blocks):
    return lax.all_to_all(blocks, "z", 0, 0, tiled=False)


def both_after(values, *others):
    return list(lax.optimization_barrier((*values, *others))[:len(values)])


def local(tokens, in_codes, in_scales, out_codes, out_scales, out_grad):
    ids = jnp.stack([lax.axis_index(name).astype(jnp.int32) for name in ("x", "z")])
    in_tiles = dequant(ids, in_codes, in_scales, True)
    out_tiles = dequant(ids, out_codes, out_scales, False)
    both = along_z(jnp.stack([tokens, out_grad]))
    both, in_tiles, out_tiles = lax.optimization_barrier((both, in_tiles, out_tiles))
    w_in = swap_z(in_tiles)
    w_out = swap_z(after(out_tiles, w_in))
    tok_own, tok_other, first = along_y(both[0])
    grad_own, grad_other, _ = along_y(after(both[1], first))
    pre_parts = swap_hidden(hidden(ids, tok_own, tok_other, w_in, False))
    grad_parts = hidden(ids, grad_own, grad_other, w_out, True)
    pre_parts = both_after(pre_parts, grad_parts[0])
    pre = add(pre_parts)
    grad_parts = swap_hidden(grad_parts)
    act_own, pre = lax.optimization_barrier((gelu_value(pre).astype(BF16), pre))
    act = gather_hidden(act_own)
    pre_grad = gather_hidden((add(grad_parts) * gelu_slope(pre)).astype(BF16))
    out_blocks = weight_grad(ids, grad_own, grad_other, act, False)
    out_moved = swap_z(out_blocks)
    out_keep, out_send = model(ids, act, w_out, False)
    pre_grad = both_after(pre_grad, out_keep, out_blocks)
    tok_keep, tok_send = model(ids, pre_grad, w_in, True)
    in_blocks = weight_grad(ids, tok_own, tok_other, both_after(pre_grad, tok_keep), True)
    in_moved = swap_z(after(in_blocks, out_moved))
    block_out = reduce_model(out_keep, out_send)
    tokens_grad = reduce_model(tok_keep, tok_send)
    out_grad_weight = assemble(ids, out_moved, False)
    in_grad = assemble(ids, in_moved, True)
    return block_out, tokens_grad, in_grad, out_grad_weight


def solution(mesh):
    grid = Mesh(mesh.devices.reshape(RING, RING, RING, 2), ("x", "z", "y", "c"))
    row, col = ("x", "z"), ("y", "c")
    in_specs = (P(col, row), P(row, col), P(row, col), P(col, row), P(col, row), P(col, row))
    out_specs = (P(col, row), P(col, row), P(row, col), P(col, row))
    return jax.shard_map(local, mesh=grid, in_specs=in_specs, out_specs=out_specs, check_vma=False)
```

```python
import functools

import jax
import jax.numpy as jnp
from jax import lax
from jax.experimental import pallas as pl
from jax.experimental.pallas import tpu as pltpu
from jax.sharding import Mesh, PartitionSpec as P

BLK = 128
RING = 4
BF16, F32 = jnp.bfloat16, jnp.float32
VMEM_LIMIT = 56 * 1024 * 1024


def gelu_value(value):
    return 0.5 * value * (1.0 + lax.erf(value * 0.7071067811865476))


def gelu_slope(value):
    cumul = 0.5 * (1.0 + lax.erf(value * 0.7071067811865476))
    return cumul + value * jnp.exp(-0.5 * value * value) * 0.3989422804014327


def shift(value, axis, step):
    size = 2 if axis == "c" else RING
    return lax.ppermute(value, axis, [(i, (i + step) % size) for i in range(size)])


def dot(left, right, dims=((1,), (0,))):
    return lax.dot_general(left, right, (dims, ((), ())), preferred_element_type=F32)


def whole(shape):
    return pl.BlockSpec(shape, lambda i, ids: (0,) * len(shape))


def call(body, ids, grid, args, in_specs, out_shape, out_specs, scratch, flops, moved):
    return pl.pallas_call(
        body,
        grid_spec=pltpu.PrefetchScalarGridSpec(
            num_scalar_prefetch=1, grid=grid, in_specs=in_specs, out_specs=out_specs, scratch_shapes=scratch
        ),
        out_shape=out_shape,
        compiler_params=pltpu.CompilerParams(
            dimension_semantics=("arbitrary",), vmem_limit_bytes=VMEM_LIMIT
        ),
        cost_estimate=pl.CostEstimate(flops=0, bytes_accessed=0, transcendentals=0),
    )(ids, *args)


def at_step(step, refs, write):
    for index, ref in enumerate(refs):
        pl.when(step == index)(functools.partial(write, ref))


def after(value, *others):
    return lax.optimization_barrier((value, *others))[0]


def dequant(ids, codes, scales, by_columns):
    rows, cols = codes.shape
    block = (rows, cols // RING) if by_columns else (rows // RING, cols)
    high, wide = block[0] // BLK, block[1] // BLK

    def body(ids_ref, scale_ref, code_ref, out):
        quarter = pl.program_id(0)
        for a in range(high):
            for b in range(wide):
                place = (slice(a * BLK, (a + 1) * BLK), slice(b * BLK, (b + 1) * BLK))
                scale = scale_ref[a, quarter * wide + b] if by_columns else scale_ref[quarter * high + a, b]
                out[(0, *place)] = (code_ref[place].astype(F32) * scale).astype(BF16)

    return call(
        body, ids, (RING,), (scales, codes),
        [pl.BlockSpec(memory_space=pltpu.SMEM),
         pl.BlockSpec(block, lambda i, ids: (0, i) if by_columns else (i, 0))],
        jax.ShapeDtypeStruct((RING, *block), BF16), pl.BlockSpec((1, *block), lambda i, ids: (i, 0, 0)), [],
        rows * cols, 4 * rows * cols,
    )


def hidden(ids, own, other, tiles, transposed):
    _, _, rows, depth = own.shape
    width = tiles.shape[1 if transposed else 2]
    step = 2 * BLK
    dims = ((1,), (1,)) if transposed else ((1,), (0,))

    def fill(ids_ref, own_ref, other_ref, left_ref):
        for k in range(RING):
            start = pl.multiple_of(lax.rem(ids_ref[1] + RING - k, RING) * depth, depth)
            for s, half in enumerate((own_ref, other_ref)):
                for j in range(RING):
                    left_ref[pl.ds((s * RING + j) * rows, rows), pl.ds(start, depth)] = half[j, k]

    def body(ids_ref, own_ref, other_ref, tile_ref, *refs):
        outs, left_ref, total_ref = refs[:RING], refs[RING], refs[RING + 1]
        pl.when(pl.program_id(0) == 0)(lambda: fill(ids_ref, own_ref, other_ref, left_ref))
        if transposed:
            right = jnp.concatenate([tile_ref[z] for z in range(RING)], axis=1)
        else:
            right = tile_ref[...].reshape(RING * depth, step)
        total_ref[...] = dot(left_ref[...], right, dims).reshape(2, RING, rows, step)
        for k in range(RING):
            quarter = lax.rem(ids_ref[0] + k, RING)
            for s in range(2):
                outs[k][s] = total_ref[s, quarter].astype(outs[k].dtype)

    tile_spec = (
        pl.BlockSpec((RING, step, depth), lambda i, ids: (0, i, 0)) if transposed
        else pl.BlockSpec((RING, depth, step), lambda i, ids: (0, 0, i))
    )
    shape = (2, rows, width)
    return call(
        body, ids, (width // step,), (own, other, tiles),
        [whole(own.shape)] * 2 + [tile_spec],
        [jax.ShapeDtypeStruct(shape, F32)] + [jax.ShapeDtypeStruct(shape, BF16)] * 3,
        [pl.BlockSpec((2, rows, step), lambda i, ids: (0, 0, i))] * RING,
        [pltpu.VMEM((2 * RING * rows, RING * depth), BF16), pltpu.VMEM((2, RING, rows, step), F32)],
        4 * own.size * width, 4 * own.size + 2 * tiles.size + 20 * rows * width,
    )


def place_parts(ids_ref, parts, whole_ref):
    rows = parts[0].shape[1]
    for k, part in enumerate(parts):
        quarter = lax.rem(ids_ref[0] + RING - k, RING)
        for s in range(2):
            whole_ref[pl.ds(pl.multiple_of((s * RING + quarter) * rows, rows), rows), :] = part[s]


def model(ids, parts, tiles, transposed):
    _, rows, width = parts[0].shape
    tokens = 2 * RING * rows
    depth = tiles.shape[1 if transposed else 2]
    dims = ((1,), (1,)) if transposed else ((1,), (0,))

    def body(ids_ref, *refs):
        hid, (first, second, keep, send, hid_ref) = refs[:RING], refs[RING:]
        pl.when(pl.program_id(0) == 0)(lambda: place_parts(ids_ref, hid, hid_ref))
        right = jnp.concatenate([first[0], second[0]], axis=0 if transposed else 1)
        total = dot(hid_ref[...], right, dims)
        for k in range(2):
            piece = total[:, k * depth:(k + 1) * depth].reshape(2, RING, rows, depth)
            keep[k] = piece[0].astype(keep.dtype)
            send[k] = piece[1].astype(send.dtype)

    shape = (RING, RING, rows, depth)
    out_spec = pl.BlockSpec((2, RING, rows, depth), lambda i, ids: (i, 0, 0, 0))
    tile_specs = [
        pl.BlockSpec((1, *tiles.shape[1:]), lambda i, ids, k=k: (lax.rem(ids[1] + RING - 2 * i - k, RING), 0, 0))
        for k in range(2)
    ]
    return call(
        body, ids, (2,), (*parts, tiles, tiles),
        [whole(p.shape) for p in parts] + tile_specs,
        [jax.ShapeDtypeStruct(shape, F32), jax.ShapeDtypeStruct(shape, BF16)],
        [out_spec] * 2,
        [pltpu.VMEM((tokens, width), BF16)],
        0, 0,
    )


def weight_grad(ids, own, other, parts, model_first):
    _, _, rows, depth = own.shape
    width = parts[0].shape[2]
    tokens = 2 * RING * rows
    shape = (depth, width) if model_first else (width, depth)

    def body(ids_ref, *refs):
        halves, hid, (out, hid_ref) = refs[:4], refs[4:4 + RING], refs[4 + RING:]
        pl.when(pl.program_id(0) == 0)(lambda: place_parts(ids_ref, hid, hid_ref))
        wide = jnp.concatenate(
            [jnp.concatenate([half[j, 0] for half in halves[2 * k:2 * k + 2] for j in range(RING)], axis=0)
             for k in range(2)], axis=1)
        if model_first:
            total = dot(wide, hid_ref[...], ((0,), (0,)))
            for k in range(2):
                out[k] = total[k * depth:(k + 1) * depth].astype(out.dtype)
        else:
            total = dot(hid_ref[...], wide, ((0,), (0,)))
            for k in range(2):
                out[k] = total[:, k * depth:(k + 1) * depth].astype(out.dtype)

    half_specs = [
        pl.BlockSpec((RING, 1, rows, depth), lambda i, ids, k=k: (0, lax.rem(ids[1] + RING - 2 * i - k, RING), 0, 0))
        for k in range(2) for _ in range(2)
    ]
    return call(
        body, ids, (2,), (own, other, own, other, *parts),
        half_specs + [whole(p.shape) for p in parts],
        jax.ShapeDtypeStruct((RING, *shape), BF16), pl.BlockSpec((2, *shape), lambda i, ids: (i, 0, 0)),
        [pltpu.VMEM((tokens, width), BF16)],
        0, 0,
    )


def assemble(ids, blocks, by_columns):
    _, rows, cols = blocks.shape
    half = rows // 2

    def body(ids_ref, block_ref, out):
        out[...] = block_ref[0].astype(F32)

    shape = (rows, RING * cols) if by_columns else (RING * rows, cols)
    return call(
        body, ids, (2 * RING,), (blocks,),
        [pl.BlockSpec((1, half, cols), lambda i, ids: (i // 2, i % 2, 0))],
        jax.ShapeDtypeStruct(shape, F32),
        pl.BlockSpec((half, cols), lambda i, ids: (i % 2, i // 2) if by_columns else (i, 0)), [],
        blocks.size, 6 * blocks.size,
    )


def along_z(value):
    return jnp.stack([value] + [shift(value, "z", k) for k in range(1, RING)], axis=1)


def along_y(value):
    moved = [shift(value, "y", k) for k in range(1, RING)]
    own = jnp.stack([value] + moved)
    return own, shift(own, "c", 1), moved[0]


def swap_hidden(parts):
    return [parts[0]] + [shift(parts[k], "x", k) for k in range(1, RING)]


def gather_hidden(value):
    return [value] + [shift(value, "x", k) for k in range(1, RING)]


def add(parts):
    total = parts[0].astype(F32)
    for part in parts[1:]:
        total = total + part.astype(F32)
    return total


def reduce_model(keep, send):
    got = shift(send, "c", 1)
    along_y = keep[:, 0] + got[:, 0].astype(F32)
    for j in range(1, RING):
        along_y = along_y + shift((keep[:, j] + got[:, j].astype(F32)).astype(BF16), "y", RING - j).astype(F32)
    total = along_y[0]
    for k in range(1, RING):
        total = total + shift(along_y[k].astype(BF16), "z", RING - k).astype(F32)
    return total.astype(BF16)


def swap_z(blocks):
    return lax.all_to_all(blocks, "z", 0, 0, tiled=False)


def both_after(values, *others):
    return list(lax.optimization_barrier((*values, *others))[:len(values)])


def local(tokens, in_codes, in_scales, out_codes, out_scales, out_grad):
    ids = jnp.stack([lax.axis_index(name).astype(jnp.int32) for name in ("x", "z")])
    in_tiles = dequant(ids, in_codes, in_scales, True)
    out_tiles = dequant(ids, out_codes, out_scales, False)
    both = along_z(jnp.stack([tokens, out_grad]))
    both, in_tiles, out_tiles = lax.optimization_barrier((both, in_tiles, out_tiles))
    w_in = swap_z(in_tiles)
    w_out = swap_z(after(out_tiles, w_in))
    tok_own, tok_other, first = along_y(both[0])
    grad_own, grad_other, _ = along_y(after(both[1], first))
    pre_parts = swap_hidden(hidden(ids, tok_own, tok_other, w_in, False))
    grad_parts = hidden(ids, grad_own, grad_other, w_out, True)
    pre_parts = both_after(pre_parts, grad_parts[0])
    pre = add(pre_parts)
    grad_parts = swap_hidden(grad_parts)
    act_own, pre = lax.optimization_barrier((gelu_value(pre).astype(BF16), pre))
    act = gather_hidden(act_own)
    pre_grad = gather_hidden((add(grad_parts) * gelu_slope(pre)).astype(BF16))
    out_blocks = weight_grad(ids, grad_own, grad_other, act, False)
    out_moved = swap_z(out_blocks)
    out_keep, out_send = model(ids, act, w_out, False)
    pre_grad = both_after(pre_grad, out_keep, out_blocks)
    tok_keep, tok_send = model(ids, pre_grad, w_in, True)
    in_blocks = weight_grad(ids, tok_own, tok_other, both_after(pre_grad, tok_keep), True)
    in_moved = swap_z(after(in_blocks, out_moved))
    block_out = reduce_model(out_keep, out_send)
    tokens_grad = reduce_model(tok_keep, tok_send)
    out_grad_weight = assemble(ids, out_moved, False)
    in_grad = assemble(ids, in_moved, True)
    return block_out, tokens_grad, in_grad, out_grad_weight


def solution(mesh):
    grid = Mesh(mesh.devices.reshape(RING, RING, RING, 2), ("x", "z", "y", "c"))
    row, col = ("x", "z"), ("y", "c")
    in_specs = (P(col, row), P(row, col), P(row, col), P(col, row), P(col, row), P(col, row))
    out_specs = (P(col, row), P(col, row), P(row, col), P(col, row))
    return jax.shard_map(local, mesh=grid, in_specs=in_specs, out_specs=out_specs, check_vma=False)
```
